256 devices in a mesh: seq: 64 (over x, z, core), dp: 4 (over y).
Axes of the slice: x: 4, y: 4, z: 8, core: 2. Of those that a mesh axis runs over, the one named last changes fastest.
Arguments:
- x_in: bfloat16 [4, 16384, 2048], P('dp', 'seq'), may hold values from -6 to 6
- gate_in: bfloat16 [4, 16384, 2048], P('dp', 'seq'), may hold values from -6 to 6
- keys_b: bfloat16 [4, 16384, 128], P('dp', 'seq'), may hold values from -6 to 6
- queries_c: bfloat16 [4, 16384, 128], P('dp', 'seq'), may hold values from -0.5 to 0.5
- decay_log: float32 [4, 32, 16384], P('dp', None, 'seq'), may hold values from -0.8 to 0
- level_mix: float32 [4, 15, 32, 16384], P('dp', None, None, 'seq'), may hold values from 0.2 to 2
- norm_gain: float32 [2048], replicated, may hold values from 0.25 to 1.75
- w_gate: bfloat16 [2048, 2816], P(None, ('seq', 'dp')), may hold values from -0.125 to 0.125
- w_up: bfloat16 [2048, 2816], P(None, ('seq', 'dp')), may hold values from -0.125 to 0.125
Outputs:
- hidden: bfloat16 [4, 16384, 2816], P('dp', 'seq')
The draws below stay inside these ranges and needn't reach their ends.
All inputs are finite; a program needn't handle non-finite values.
Results may differ from the reference program's by a relative error of at most 0.0078.
Values may be sent and summed in bfloat16 or wider, within the bound.
No kernel may reach another device: no remote copies, remote signals or barrier semaphores. Data moves between devices by JAX's collectives and lax.ppermute only.
A program may use at most 128 MiB of HBM per device.

```python
import math
import jax
import jax.numpy as jnp
from jax import lax

HEADS = 32
HEAD_DIM = 64
STATE = 128
FF = 2816
SPAN = 256
SPAN_BITS = 8
D = 2048
TOK_DEV = 256
SEQUENCE_TOKENS = 16384
SEQUENCE_COUNT = 4
FENWICK_LEVELS = 15


def draw_decay_log(key, part):
    key = jax.random.fold_in(key, 11)
    k_fast, k_slow, k_quick, k_dev, k_tok, key_position, k_loss = jax.random.split(key, 7)
    devices = SEQUENCE_TOKENS // TOK_DEV
    fast = jax.random.uniform(k_fast, (SEQUENCE_COUNT, HEADS, 1)) < 0.5
    tok_scale = jnp.exp(jax.random.uniform(k_tok, (SEQUENCE_COUNT, HEADS, SEQUENCE_TOKENS), minval=math.log(0.5), maxval=math.log(1.5)))
    slow_rate = jax.random.uniform(k_slow, (SEQUENCE_COUNT, HEADS, 1), minval=0.1, maxval=0.35) / SEQUENCE_TOKENS
    quick_rate = jnp.exp(jax.random.uniform(k_quick, (SEQUENCE_COUNT, HEADS, 1), minval=math.log(1.0 / 50.0), maxval=math.log(1.0 / 30.0)))
    base_rate = jnp.where(fast, quick_rate, slow_rate)
    dev_scale = jnp.exp(jax.random.uniform(k_dev, (SEQUENCE_COUNT, HEADS, devices), minval=math.log(0.5), maxval=math.log(1.5)))
    dev_scale = jnp.repeat(dev_scale, TOK_DEV, axis=2)
    surge_position = jax.random.randint(key_position, (SEQUENCE_COUNT, 1, 1, 2), 0, SEQUENCE_TOKENS)
    level_match = jnp.any(jnp.arange(SEQUENCE_TOKENS)[None, None, :, None] == surge_position, axis=-1)
    loss = jax.random.uniform(k_loss, (SEQUENCE_COUNT, HEADS, SEQUENCE_TOKENS), minval=0.22, maxval=0.69)
    return -(base_rate * dev_scale * tok_scale) - jnp.where(level_match, loss, 0.0)


def shard_levels(own_key, extent, cuts, least, largest):
    gain, own = 1.0, jax.random.fold_in(own_key, 6)
    for dim, blocks in cuts:
        draws = jnp.exp(jax.random.uniform(jax.random.fold_in(own, dim), (blocks,), jnp.float32, least / len(cuts), largest / len(cuts)))
        gain = gain * jnp.repeat(draws, extent[dim] // blocks).reshape([-1 if axis == dim else 1 for axis in range(len(extent))])
    return gain


def bell_draw(own_key, dims, deviation, most, shards=(), kind=jnp.bfloat16):
    array = deviation * jax.random.normal(own_key, dims, jnp.float32)
    if shards:
        array = array * shard_levels(own_key, dims, shards, -0.22, 0.18)
    return jnp.clip(array, -most, most).astype(kind)


def setup_inputs(seed: int = 0) -> dict:
    arg_keys = jax.random.split(jax.random.key(seed), 10)
    x_in = bell_draw(arg_keys[0], (SEQUENCE_COUNT, SEQUENCE_TOKENS, D), 1.0, 6.0, ((0, 4), (1, 64)))
    gate_in = bell_draw(arg_keys[1], (SEQUENCE_COUNT, SEQUENCE_TOKENS, D), 1.0, 6.0, ((0, 4), (1, 64)))
    keys_b = bell_draw(arg_keys[2], (SEQUENCE_COUNT, SEQUENCE_TOKENS, STATE), 1.0, 6.0, ((0, 4), (1, 64)))
    queries_c = bell_draw(arg_keys[3], (SEQUENCE_COUNT, SEQUENCE_TOKENS, STATE), STATE ** -0.5, 0.5, ((0, 4), (1, 64)))
    decay_log = draw_decay_log(jax.random.fold_in(arg_keys[9], 71), 0)
    level_mix = jnp.clip(jnp.exp(math.log(2.0) - 2.3025851 * jax.random.uniform(arg_keys[5], (SEQUENCE_COUNT, FENWICK_LEVELS, HEADS, SEQUENCE_TOKENS), jnp.float32) ** shard_levels(arg_keys[5], (SEQUENCE_COUNT, FENWICK_LEVELS, HEADS, SEQUENCE_TOKENS), ((0, 4), (3, 64)), -0.2, 0.2)), 0.2, 2.0)
    norm_gain = jnp.clip(1.0 + 0.15 * jax.random.normal(arg_keys[6], (D,), jnp.float32), 0.25, 1.75)
    w_gate = bell_draw(arg_keys[7], (D, FF), D ** -0.5, 0.125, ((1, 256),))
    w_up = bell_draw(arg_keys[8], (D, FF), D ** -0.5, 0.125, ((1, 256),))
    return {"x_in": x_in, "gate_in": gate_in, "keys_b": keys_b, "queries_c": queries_c, "decay_log": decay_log, "level_mix": level_mix, "norm_gain": norm_gain, "w_gate": w_gate, "w_up": w_up}


EPS = 1e-05
HIGH = lax.Precision.HIGHEST

def top_bit(values):
    powers = jnp.arange(1, 31, dtype=jnp.int32)
    return lax.optimization_barrier(jnp.sum(values[..., None] >> powers > 0, axis=-1)).astype(jnp.int32)

def rounded(values):
    return lax.optimization_barrier(values.astype(jnp.bfloat16)).astype(jnp.float32)

def block_inner(x_blk, b_blk, c_blk, a_blk, mix_low):
    length = a_blk.shape[1]
    inner_count = mix_low.shape[0]
    running = jnp.cumsum(a_blk, axis=1)
    position = jnp.arange(length, dtype=jnp.int32)
    differ = position[:, None] ^ position[None, :]
    level_table = jnp.where(differ > 0, top_bit(differ) + 1, 0)
    level_picks = (level_table[None] == jnp.arange(inner_count, dtype=jnp.int32)[:, None, None]).astype(jnp.float32)
    chosen = jnp.einsum('lht,lts->hts', mix_low, level_picks, precision=HIGH)
    causal_mask = position[:, None] >= position[None, :]
    log_gap = jnp.where(causal_mask[None], running[:, :, None] - running[:, None, :], -jnp.inf)
    scores = jnp.dot(c_blk, b_blk.T, preferred_element_type=jnp.float32)
    weights = rounded(chosen * jnp.exp(log_gap) * scores[None])
    local_part = jnp.einsum('hts,shp->thp', weights, x_blk.astype(jnp.float32), precision=HIGH)
    tail_decay = jnp.exp(running[:, -1:] - running)
    scaled_keys = rounded(tail_decay.T[:, :, None] * b_blk[:, None, :].astype(jnp.float32))
    block_state = jnp.einsum('shn,shp->hnp', scaled_keys, x_blk.astype(jnp.float32), precision=HIGH)
    return (local_part, block_state, running)

def block_distant(c_blk, running, mix_high, levels):
    growth = jnp.exp(running)
    distant_sum = jnp.zeros((c_blk.shape[0], running.shape[0], levels[0].shape[2]), jnp.float32)
    for level_rank in range(len(levels)):
        level_scale = (mix_high[level_rank] * growth).T
        product = jnp.einsum('tn,hnp->thp', c_blk.astype(jnp.float32), rounded(levels[level_rank]), precision=HIGH)
        distant_sum = distant_sum + level_scale[:, :, None] * product
    return distant_sum

def reference(x_in, gate_in, keys_b, queries_c, decay_log, level_mix, norm_gain, w_gate, w_up):
    span_count = SEQUENCE_TOKENS // SPAN
    inner_count = SPAN_BITS + 1
    outer_count = FENWICK_LEVELS - inner_count

    def per_sequence(items):
        x_seq, z_seq, b_seq, c_seq, a_seq, mix_seq = items
        x_blocks = x_seq.reshape(span_count, SPAN, HEADS, HEAD_DIM)
        b_blocks = b_seq.reshape(span_count, SPAN, STATE)
        c_blocks = c_seq.reshape(span_count, SPAN, STATE)
        a_blocks = a_seq.reshape(HEADS, span_count, SPAN).transpose(1, 0, 2)
        mix_blocks = mix_seq.reshape(FENWICK_LEVELS, HEADS, span_count, SPAN).transpose(2, 0, 1, 3)

        def first_pass(block_items):
            x_blk, b_blk, c_blk, a_blk, mix_blk = block_items
            return block_inner(x_blk, b_blk, c_blk, a_blk, mix_blk[:inner_count])
        local_parts, block_states, runnings = lax.map(first_pass, (x_blocks, b_blocks, c_blocks, a_blocks, mix_blocks))
        block_decays = runnings[:, :, -1]
        before = jnp.concatenate([jnp.zeros((1, HEADS), jnp.float32), jnp.cumsum(block_decays, axis=0)], axis=0)
        span_ids = jnp.arange(span_count, dtype=jnp.int32)

        def second_pass(block_items):
            here, c_blk, running, mix_blk = block_items
            level_ids = inner_count + top_bit(here ^ span_ids)
            earlier = span_ids < here
            log_gap = before[here][None, :] - before[1:]
            levels = []
            for level_rank in range(outer_count):
                keep = earlier & (level_ids == inner_count + level_rank)
                factor = jnp.exp(jnp.where(keep[:, None], log_gap, -jnp.inf))
                levels.append(jnp.einsum('ih,ihnp->hnp', factor, block_states, precision=HIGH))
            return block_distant(c_blk, running, mix_blk[inner_count:], levels)
        distant = lax.map(second_pass, (span_ids, c_blocks, runnings, mix_blocks))
        mixed = (local_parts + distant).reshape(SEQUENCE_TOKENS, HEADS * HEAD_DIM)
        gated = mixed * jax.nn.silu(z_seq.astype(jnp.float32))
        normed = (gated * lax.rsqrt(lax.optimization_barrier(jnp.mean(gated * gated, axis=-1, keepdims=True)) + EPS) * norm_gain).astype(jnp.bfloat16)
        gate_pre = jnp.dot(normed, w_gate, preferred_element_type=jnp.float32)
        up_pre = jnp.dot(normed, w_up, preferred_element_type=jnp.float32)
        return (jax.nn.silu(gate_pre) * up_pre).astype(jnp.bfloat16)
    return lax.map(per_sequence, (x_in, gate_in, keys_b, queries_c, decay_log, level_mix))
```

```python
import jax
import jax.numpy as jnp
from jax import lax
from jax.sharding import Mesh
from jax.sharding import PartitionSpec as P

SPAN = 256
SPAN_BITS = 8
EPS = 1e-05
HIGH = lax.Precision.HIGHEST
SEQ = ("x", "z", "core")
STEPS = (("z", 1), ("z", 2), ("z", 4), ("x", 1), ("x", 2))
HEAD_DIM = 64


def swapped(value, axis, mask):
    return lax.ppermute(value, axis, [(i, i ^ mask) for i in range(lax.axis_size(axis))])


def shifted(value, axis, step):
    count = lax.axis_size(axis)
    return lax.ppermute(value, axis, [(i, (i + step) % count) for i in range(count)])


def top_bit(values):
    powers = jnp.arange(1, 31, dtype=jnp.int32)
    return jnp.sum(values[..., None] >> powers > 0, axis=-1)


def local_mix(x_blk, b_blk, c_blk, running, mix_low):
    length = running.shape[1]
    inner_count = mix_low.shape[0]
    position = jnp.arange(length, dtype=jnp.int32)
    differ = position[:, None] ^ position[None, :]
    level_table = jnp.where(differ > 0, top_bit(differ) + 1, 0)
    level_picks = (
        level_table[None] == jnp.arange(inner_count, dtype=jnp.int32)[:, None, None]
    ).astype(jnp.float32)
    chosen = jnp.einsum("lht,lts->hts", mix_low, level_picks, precision=HIGH)
    causal_mask = position[:, None] >= position[None, :]
    log_gap = jnp.where(causal_mask[None], running[:, :, None] - running[:, None, :], -jnp.inf)
    scores = jnp.dot(c_blk, b_blk.T, preferred_element_type=jnp.float32)
    weights = (chosen * jnp.exp(log_gap) * scores[None]).astype(jnp.bfloat16)
    return jnp.einsum("hts,shp->thp", weights, x_blk, preferred_element_type=jnp.float32)


def packed(state, decay, kind):
    heads, width, size = state.shape
    top = lax.reduce_precision(decay, 8, 7)
    middle = lax.reduce_precision(decay - top, 8, 7)
    low = lax.reduce_precision(decay - top - middle, 8, 7)
    tail = jnp.stack([top, middle, low] + [jnp.zeros_like(top)] * 5)
    tail = jnp.pad(tail, ((0, 0), (0, size - decay.shape[0])))
    rows = jnp.concatenate([state.reshape(heads * width, size), tail])
    return rows.astype(kind)


def unpacked(rows, heads):
    size = rows.shape[1]
    tail = rows[-8:, :heads].astype(jnp.float32)
    state = rows[:-8].reshape(-1, HEAD_DIM, size)
    return state.astype(jnp.float32), tail[0] + tail[1] + tail[2]


def gathered_weights(w_gate, w_up, core, row):
    gate, up = w_gate.T, w_up.T
    keep = jnp.where(core == 0, gate, up)
    other = swapped(jnp.where(core == 0, up, gate), "core", 1)
    pair = jnp.stack([jnp.where(core == 0, keep, other), jnp.where(core == 0, other, keep)])
    ring = [pair, shifted(pair, "dp", -1), shifted(pair, "dp", 2), shifted(pair, "dp", 1)]
    placed = []
    for index in range(4):
        turn = (index - row) % 4
        value = ring[0]
        for step in range(1, 4):
            value = jnp.where(turn == step, ring[step], value)
        placed.append(value)
    block = jnp.stack(placed, axis=1).reshape(-1, gate.shape[1])
    return lax.all_gather(block, ("x", "z"), axis=0, tiled=True)


def per_device(x_in, gate_in, keys_b, queries_c, decay_log, level_mix, norm_gain, w_gate, w_up):
    tokens, width = x_in.shape[1:]
    heads = decay_log.shape[1]
    head_dim = HEAD_DIM
    inner = SPAN_BITS + 1
    core = lax.axis_index("core")
    here = (lax.axis_index("x") * lax.axis_size("z") + lax.axis_index("z")) * 2 + core
    mine = gathered_weights(w_gate, w_up, core, lax.axis_index("dp"))
    other = swapped(mine, "core", 1)

    x_blk = x_in[0].reshape(tokens, heads, head_dim)
    b_blk, c_blk = keys_b[0], queries_c[0]
    mix = level_mix[0]
    running = jnp.cumsum(decay_log[0], axis=1)
    decay = running[:, -1]
    tail_decay = jnp.exp(running[:, -1:] - running)
    scaled_keys = (tail_decay.T[:, :, None] * b_blk[:, None, :]).astype(jnp.bfloat16)
    state = jnp.einsum("shn,shp->hpn", scaled_keys, x_blk, preferred_element_type=jnp.float32)

    half = heads // 2
    their_state, their_decay = unpacked(swapped(packed(state, decay, jnp.float32), "core", 1), heads)
    first_level = their_state.astype(jnp.bfloat16)
    lower_state = jnp.where(core == 0, state, their_state)
    upper_state = jnp.where(core == 0, their_state, state)
    upper_decay = jnp.where(core == 0, their_decay, decay)
    summary = jnp.exp(upper_decay)[:, None, None] * lower_state + upper_state
    summary = lax.dynamic_slice_in_dim(summary, core * half, half)
    total = decay + their_decay
    prefix = jnp.zeros_like(total)
    upper, lead = [core == 1], [prefix]
    prefix = jnp.where(core == 1, their_decay, 0.0)
    levels = []
    for bit, (axis, mask) in enumerate(STEPS, 1):
        received = swapped(packed(summary, total, jnp.bfloat16), axis, mask)
        levels.append(received[:-8])
        their_state, their_decay = unpacked(received, heads)
        is_upper = here >> bit & 1 == 1
        upper.append(is_upper)
        lead.append(prefix)
        if bit < len(STEPS):
            lower_state = jnp.where(is_upper, their_state, summary)
            upper_state = jnp.where(is_upper, summary, their_state)
            upper_decay = jnp.where(is_upper, total, their_decay)
            gain = lax.dynamic_slice_in_dim(jnp.exp(upper_decay), core * half, half)
            summary = gain[:, None, None] * lower_state + upper_state
            prefix = jnp.where(is_upper, prefix + their_decay, prefix)
            total = total + their_decay

    def whole(own):
        own = jnp.stack(own).reshape(len(own), half, head_dim, -1)
        theirs = swapped(own, "core", 1)
        pair = (jnp.where(core == 0, own, theirs), jnp.where(core == 0, theirs, own))
        return list(jnp.concatenate(pair, axis=1))

    all_levels = [first_level] + whole(levels[:3]) + whole(levels[3:])
    mixed = local_mix(x_blk, b_blk, c_blk, running, mix[:inner])
    for rank, level in enumerate(all_levels):
        growth = jnp.where(upper[rank], jnp.exp(running + lead[rank][:, None]), 0.0)
        scale = (mix[inner + rank] * growth).T
        product = jnp.einsum("tn,hpn->thp", c_blk, level, preferred_element_type=jnp.float32)
        mixed = mixed + scale[:, :, None] * product
    mixed = mixed.reshape(tokens, width)
    gated = mixed * jax.nn.silu(gate_in[0].astype(jnp.float32))
    normed = (
        gated * lax.rsqrt(jnp.mean(gated * gated, axis=-1, keepdims=True) + EPS) * norm_gain
    ).astype(jnp.bfloat16)
    dims = (((1,), (1,)), ((), ()))
    own_part = lax.dot_general(normed, mine, dims, preferred_element_type=jnp.float32)
    other_part = lax.dot_general(normed, other, dims, preferred_element_type=jnp.float32)
    gate_pre = jnp.where(core == 0, own_part, other_part)
    up_pre = jnp.where(core == 0, other_part, own_part)
    return (jax.nn.silu(gate_pre) * up_pre).astype(jnp.bfloat16)[None]


def solution(mesh):
    whole = Mesh(mesh.devices.reshape(4, 8, 2, 4), ("x", "z", "core", "dp"))
    in_specs = (
        P("dp", SEQ, None),
        P("dp", SEQ, None),
        P("dp", SEQ, None),
        P("dp", SEQ, None),
        P("dp", None, SEQ),
        P("dp", None, None, SEQ),
        P(),
        P(None, SEQ + ("dp",)),
        P(None, SEQ + ("dp",)),
    )
    return jax.shard_map(
        per_device, mesh=whole, in_specs=in_specs, out_specs=P("dp", SEQ, None), check_vma=False
    )
```

```python
import jax
import jax.numpy as jnp
from jax import lax
from jax.sharding import Mesh
from jax.sharding import PartitionSpec as P

SPAN = 256
SPAN_BITS = 8
EPS = 1e-05
HIGH = lax.Precision.HIGHEST
SEQ = ("x", "z", "core")
STEPS = (("z", 1), ("z", 2), ("z", 4), ("x", 1), ("x", 2))
HEAD_DIM = 64


def swapped(value, axis, mask):
    return lax.ppermute(value, axis, [(i, i ^ mask) for i in range(lax.axis_size(axis))])


def shifted(value, axis, step):
    count = lax.axis_size(axis)
    return lax.ppermute(value, axis, [(i, (i + step) % count) for i in range(count)])


def top_bit(values):
    powers = jnp.arange(1, 31, dtype=jnp.int32)
    return jnp.sum(values[..., None] >> powers > 0, axis=-1)


def local_mix(x_blk, b_blk, c_blk, running, mix_low):
    length = running.shape[1]
    inner_count = mix_low.shape[0]
    position = jnp.arange(length, dtype=jnp.int32)
    differ = position[:, None] ^ position[None, :]
    level_table = jnp.where(differ > 0, top_bit(differ) + 1, 0)
    level_picks = (
        level_table[None] == jnp.arange(inner_count, dtype=jnp.int32)[:, None, None]
    ).astype(jnp.float32)
    chosen = jnp.einsum("lht,lts->hts", mix_low, level_picks, precision=HIGH)
    causal_mask = position[:, None] >= position[None, :]
    log_gap = jnp.where(causal_mask[None], running[:, :, None] - running[:, None, :], -jnp.inf)
    scores = jnp.dot(c_blk, b_blk.T, preferred_element_type=jnp.float32)
    weights = (chosen * jnp.exp(log_gap) * scores[None]).astype(jnp.bfloat16)
    return jnp.einsum("hts,shp->thp", weights, x_blk, preferred_element_type=jnp.float32)


def packed(state, decay, kind):
    heads, width, size = state.shape
    top = lax.reduce_precision(decay, 8, 7)
    middle = lax.reduce_precision(decay - top, 8, 7)
    low = lax.reduce_precision(decay - top - middle, 8, 7)
    tail = jnp.stack([top, middle, low] + [jnp.zeros_like(top)] * 5)
    tail = jnp.pad(tail, ((0, 0), (0, size - decay.shape[0])))
    rows = jnp.concatenate([state.reshape(heads * width, size), tail])
    return rows.astype(kind)


def unpacked(rows, heads):
    size = rows.shape[1]
    tail = rows[-8:, :heads].astype(jnp.float32)
    state = rows[:-8].reshape(-1, HEAD_DIM, size)
    return state.astype(jnp.float32), tail[0] + tail[1] + tail[2]


def gathered_weights(w_gate, w_up, core, row):
    gate, up = w_gate.T, w_up.T
    keep = jnp.where(core == 0, gate, up)
    other = swapped(jnp.where(core == 0, up, gate), "core", 1)
    pair = jnp.stack([jnp.where(core == 0, keep, other), jnp.where(core == 0, other, keep)])
    ring = [pair, shifted(pair, "dp", -1), shifted(pair, "dp", 2), shifted(pair, "dp", 1)]
    placed = []
    for index in range(4):
        turn = (index - row) % 4
        value = ring[0]
        for step in range(1, 4):
            value = jnp.where(turn == step, ring[step], value)
        placed.append(value)
    block = jnp.stack(placed, axis=1).reshape(-1, gate.shape[1])
    return lax.all_gather(block, ("x", "z"), axis=0, tiled=True)


def per_device(x_in, gate_in, keys_b, queries_c, decay_log, level_mix, norm_gain, w_gate, w_up):
    tokens, width = x_in.shape[1:]
    heads = decay_log.shape[1]
    head_dim = HEAD_DIM
    inner = SPAN_BITS + 1
    core = lax.axis_index("core")
    here = (lax.axis_index("x") * lax.axis_size("z") + lax.axis_index("z")) * 2 + core
    mine = gathered_weights(w_gate, w_up, core, lax.axis_index("dp"))

    x_blk = x_in[0].reshape(tokens, heads, head_dim)
    b_blk, c_blk = keys_b[0], queries_c[0]
    mix = level_mix[0]
    running = jnp.cumsum(decay_log[0], axis=1)
    decay = running[:, -1]
    tail_decay = jnp.exp(running[:, -1:] - running)
    scaled_keys = (tail_decay.T[:, :, None] * b_blk[:, None, :]).astype(jnp.bfloat16)
    state = jnp.einsum("shn,shp->hpn", scaled_keys, x_blk, preferred_element_type=jnp.float32)

    half = heads // 2
    their_state, their_decay = unpacked(swapped(packed(state, decay, jnp.float32), "core", 1), heads)
    first_level = their_state.astype(jnp.bfloat16)
    lower_state = jnp.where(core == 0, state, their_state)
    upper_state = jnp.where(core == 0, their_state, state)
    upper_decay = jnp.where(core == 0, their_decay, decay)
    summary = jnp.exp(upper_decay)[:, None, None] * lower_state + upper_state
    summary = lax.dynamic_slice_in_dim(summary, core * half, half)
    total = decay + their_decay
    prefix = jnp.zeros_like(total)
    upper, lead = [core == 1], [prefix]
    prefix = jnp.where(core == 1, their_decay, 0.0)
    levels = []
    for bit, (axis, mask) in enumerate(STEPS, 1):
        received = swapped(packed(summary, total, jnp.bfloat16), axis, mask)
        levels.append(received[:-8])
        their_state, their_decay = unpacked(received, heads)
        is_upper = here >> bit & 1 == 1
        upper.append(is_upper)
        lead.append(prefix)
        if bit < len(STEPS):
            lower_state = jnp.where(is_upper, their_state, summary)
            upper_state = jnp.where(is_upper, summary, their_state)
            upper_decay = jnp.where(is_upper, total, their_decay)
            gain = lax.dynamic_slice_in_dim(jnp.exp(upper_decay), core * half, half)
            summary = gain[:, None, None] * lower_state + upper_state
            prefix = jnp.where(is_upper, prefix + their_decay, prefix)
            total = total + their_decay

    def whole(own):
        own = jnp.stack(own).reshape(len(own), half, head_dim, -1)
        theirs = swapped(own, "core", 1)
        pair = (jnp.where(core == 0, own, theirs), jnp.where(core == 0, theirs, own))
        return list(jnp.concatenate(pair, axis=1))

    all_levels = [first_level] + whole(levels[:3]) + whole(levels[3:])
    mixed = local_mix(x_blk, b_blk, c_blk, running, mix[:inner])
    for rank, level in enumerate(all_levels):
        growth = jnp.where(upper[rank], jnp.exp(running + lead[rank][:, None]), 0.0)
        scale = (mix[inner + rank] * growth).T
        product = jnp.einsum("tn,hpn->thp", c_blk, level, preferred_element_type=jnp.float32)
        mixed = mixed + scale[:, :, None] * product
    mixed = mixed.reshape(tokens, width)
    gated = mixed * jax.nn.silu(gate_in[0].astype(jnp.float32))
    normed = (
        gated * lax.rsqrt(jnp.mean(gated * gated, axis=-1, keepdims=True) + EPS) * norm_gain
    ).astype(jnp.bfloat16)
    normed = lax.optimization_barrier(normed)
    dims = (((1,), (1,)), ((), ()))
    theirs = swapped(normed, "core", 1)
    sent = lax.dot_general(theirs, mine, dims, preferred_element_type=jnp.float32)
    other_part = swapped(sent, "core", 1)
    own_part = lax.dot_general(normed, mine, dims, preferred_element_type=jnp.float32)
    gate_pre = jnp.where(core == 0, own_part, other_part)
    up_pre = jnp.where(core == 0, other_part, own_part)
    return (jax.nn.silu(gate_pre) * up_pre).astype(jnp.bfloat16)[None]


def solution(mesh):
    whole = Mesh(mesh.devices.reshape(4, 8, 2, 4), ("x", "z", "core", "dp"))
    in_specs = (
        P("dp", SEQ, None),
        P("dp", SEQ, None),
        P("dp", SEQ, None),
        P("dp", SEQ, None),
        P("dp", None, SEQ),
        P("dp", None, None, SEQ),
        P(),
        P(None, SEQ + ("dp",)),
        P(None, SEQ + ("dp",)),
    )
    return jax.shard_map(
        per_device, mesh=whole, in_specs=in_specs, out_specs=P("dp", SEQ, None), check_vma=False
    )
```

```python
import jax
import jax.numpy as jnp
import numpy as np
from jax import lax
from jax.experimental import pallas as pl
from jax.experimental.pallas import tpu as pltpu
from jax.sharding import Mesh
from jax.sharding import PartitionSpec as P

SPAN = 256
SPAN_BITS = 8
EPS = 1e-05
HIGH = lax.Precision.HIGHEST
SEQ = ("x", "z", "core")
STEPS = (("z", 1), ("z", 2), ("z", 4), ("x", 1), ("x", 2))
HEAD_DIM = 64
FIRST = 7
TURNS = (0, 3, 1, 2)


def swapped(value, axis, mask):
    return lax.ppermute(value, axis, [(i, i ^ mask) for i in range(lax.axis_size(axis))])


def shifted(value, axis, step):
    count = lax.axis_size(axis)
    return lax.ppermute(value, axis, [(i, (i + step) % count) for i in range(count)])


def top_bit(values):
    powers = jnp.arange(1, 31, dtype=jnp.int32)
    return jnp.sum(values[..., None] >> powers > 0, axis=-1)


def local_mix(x_blk, b_blk, c_blk, running, mix_low):
    length = running.shape[1]
    inner_count = mix_low.shape[0]
    position = jnp.arange(length, dtype=jnp.int32)
    differ = position[:, None] ^ position[None, :]
    level_table = jnp.where(differ > 0, top_bit(differ) + 1, 0)
    level_picks = (
        level_table[None] == jnp.arange(inner_count, dtype=jnp.int32)[:, None, None]
    ).astype(jnp.float32)
    chosen = jnp.einsum("lht,lts->hts", mix_low, level_picks, precision=HIGH)
    causal_mask = position[:, None] >= position[None, :]
    log_gap = jnp.where(causal_mask[None], running[:, :, None] - running[:, None, :], -jnp.inf)
    scores = jnp.dot(c_blk, b_blk.T, preferred_element_type=jnp.float32)
    weights = (chosen * jnp.exp(log_gap) * scores[None]).astype(jnp.bfloat16)
    return jnp.einsum("hts,shp->thp", weights, x_blk, preferred_element_type=jnp.float32)


def packed(state, decay, kind):
    heads, width, size = state.shape
    top = lax.reduce_precision(decay, 8, 7)
    middle = lax.reduce_precision(decay - top, 8, 7)
    low = lax.reduce_precision(decay - top - middle, 8, 7)
    tail = jnp.stack([top, middle, low] + [jnp.zeros_like(top)] * 5)
    tail = jnp.pad(tail, ((0, 0), (0, size - decay.shape[0])))
    rows = jnp.concatenate([state.reshape(heads * width, size), tail])
    return rows.astype(kind)


def unpacked(rows, heads):
    size = rows.shape[1]
    tail = rows[-8:, :heads].astype(jnp.float32)
    state = rows[:-8].reshape(-1, HEAD_DIM, size)
    return state.astype(jnp.float32), tail[0] + tail[1] + tail[2]


def gathered_weights(w_gate, w_up, core):
    gate, up = w_gate.T, w_up.T
    depth = gate.shape[1]
    keep = jnp.where(core == 0, gate, up)
    other = swapped(jnp.where(core == 0, up, gate), "core", 1)
    pair = jnp.stack([jnp.where(core == 0, keep, other), jnp.where(core == 0, other, keep)])
    first = pair[:, :FIRST].reshape(1, -1, depth)
    ring = [first] + [shifted(first, "dp", -step) for step in range(1, 4)]
    block = jnp.concatenate(ring).reshape(-1, depth)
    main = lax.all_gather(block, ("x", "z"), axis=0, tiled=True)

    rest = pair[:, FIRST:].reshape(-1, depth)
    for axis, mask in STEPS:
        if (axis, mask) == STEPS[-1]:
            mark = rest[:1, :1].astype(jnp.float32) * 0
        theirs = swapped(rest, axis, mask)
        is_low = lax.axis_index(axis) & mask == 0
        rest = jnp.concatenate([jnp.where(is_low, rest, theirs), jnp.where(is_low, theirs, rest)])
    middle = rest.shape[0] // 2
    before, after = shifted(rest, "dp", 1), shifted(rest, "dp", -1)
    far_low = shifted(before[:middle], "dp", 1)
    far_high = shifted(after[middle:], "dp", -1)
    return main, [rest, before, after, far_low, far_high], mark


def rest_kernel(theirs, own, *refs):
    *weights, sent, kept = refs
    start = 0
    for piece in weights:
        columns = slice(start, start + piece.shape[0])
        start += piece.shape[0]
        for source, out in ((theirs, sent), (own, kept)):
            out[:, columns] = lax.dot_general(
                source[...], piece[...], (((1,), (1,)), ((), ())), preferred_element_type=jnp.float32
            )


def rest_product(theirs, own, pieces):
    tokens, depth = own.shape
    columns = sum(piece.shape[0] for piece in pieces)
    shape = jax.ShapeDtypeStruct((tokens, columns), jnp.float32)
    return pl.pallas_call(
        rest_kernel,
        out_shape=(shape, shape),
        compiler_params=pltpu.CompilerParams(vmem_limit_bytes=40 * 2**20),
        cost_estimate=pl.CostEstimate(
            flops=4 * tokens * columns * depth, bytes_accessed=8 * 2**20, transcendentals=0
        ),
    )(theirs, own, *pieces)


def column_order(row):
    chip, turn, core, unit = np.meshgrid(*map(np.arange, (16, 4, 2, FIRST)), indexing="ij")
    base = [(chip * 88 + core * 44 + unit).ravel()]
    turns = [turn.ravel()]
    turn, chip, core, unit = np.meshgrid(*map(np.arange, (4, 16, 2, 11 - FIRST)), indexing="ij")
    base.append((chip * 88 + core * 44 + FIRST + unit).ravel())
    turns.append(np.array(TURNS)[turn].ravel())
    base, turns = np.concatenate(base), np.concatenate(turns)
    place = jnp.asarray(base, jnp.int32) + (row + jnp.asarray(turns, jnp.int32)) % 4 * 11
    columns = jnp.arange(base.size, dtype=jnp.int32)
    return (place[:, None] == columns[None, :]).astype(jnp.bfloat16)


def finish_kernel(core_ref, own_a, other_a, own_b, other_b, order, out, held):
    half = pl.program_id(0)
    is_gate = core_ref[0] == 0

    def hidden(own, other):
        gate_pre = jnp.where(is_gate, own, other)
        up_pre = jnp.where(is_gate, other, own)
        return (jax.nn.silu(gate_pre) * up_pre).astype(jnp.bfloat16)

    wide = own_a.shape[1]
    held[:, :wide] = hidden(own_a[...], other_a[...])
    for turn in range(4):
        columns = pl.ds(pl.multiple_of(turn * 256 + half * 128, 128), 128)
        held[:, wide + turn * 128 : wide + (turn + 1) * 128] = hidden(
            own_b[:, columns], other_b[:, columns]
        )
    out[...] = jnp.dot(held[...], order[...], preferred_element_type=jnp.float32).astype(out.dtype)


def finished(core, own_a, other_a, own_b, other_b, order):
    tokens = own_a.shape[0]
    size = order.shape[0]
    wide = pl.BlockSpec((tokens, own_a.shape[1] // 2), lambda h, c: (0, h))
    whole = pl.BlockSpec((tokens, own_b.shape[1]), lambda h, c: (0, 0))
    return pl.pallas_call(
        finish_kernel,
        grid_spec=pltpu.PrefetchScalarGridSpec(
            num_scalar_prefetch=1,
            grid=(2,),
            in_specs=[wide, wide, whole, whole, pl.BlockSpec((size, size), lambda h, c: (0, 0))],
            out_specs=pl.BlockSpec((tokens, size), lambda h, c: (0, h)),
            scratch_shapes=[pltpu.VMEM((tokens, size), jnp.bfloat16)],
        ),
        out_shape=jax.ShapeDtypeStruct((tokens, 2 * size), jnp.bfloat16),
        compiler_params=pltpu.CompilerParams(vmem_limit_bytes=40 * 2**20),
        cost_estimate=pl.CostEstimate(
            flops=4 * tokens * size * size, bytes_accessed=24 * 2**20, transcendentals=2 * tokens * size
        ),
    )(core[None], own_a, other_a, own_b, other_b, order)


def per_device(x_in, gate_in, keys_b, queries_c, decay_log, level_mix, norm_gain, w_gate, w_up):
    tokens, width = x_in.shape[1:]
    heads = decay_log.shape[1]
    head_dim = HEAD_DIM
    inner = SPAN_BITS + 1
    core = lax.axis_index("core")
    here = (lax.axis_index("x") * lax.axis_size("z") + lax.axis_index("z")) * 2 + core
    main, rest, mark = gathered_weights(w_gate, w_up, core)

    x_blk = x_in[0].reshape(tokens, heads, head_dim)
    b_blk, c_blk = keys_b[0], queries_c[0]
    mix = level_mix[0]
    running = jnp.cumsum(decay_log[0], axis=1)
    decay = running[:, -1]
    tail_decay = jnp.exp(running[:, -1:] - running)
    scaled_keys = (tail_decay.T[:, :, None] * b_blk[:, None, :]).astype(jnp.bfloat16)
    state = jnp.einsum("shn,shp->hpn", scaled_keys, x_blk, preferred_element_type=jnp.float32)

    half = heads // 2
    their_state, their_decay = unpacked(swapped(packed(state, decay, jnp.float32), "core", 1), heads)
    first_level = their_state.astype(jnp.bfloat16)
    lower_state = jnp.where(core == 0, state, their_state)
    upper_state = jnp.where(core == 0, their_state, state)
    upper_decay = jnp.where(core == 0, their_decay, decay)
    summary = jnp.exp(upper_decay)[:, None, None] * lower_state + upper_state
    summary = lax.dynamic_slice_in_dim(summary, core * half, half)
    total = decay + their_decay
    prefix = jnp.zeros_like(total)
    upper, lead = [core == 1], [prefix]
    prefix = jnp.where(core == 1, their_decay, 0.0)
    levels = []
    start = core * half
    quarter = half // 2
    odd = lax.axis_index("z") & 1
    for bit, (axis, mask) in enumerate(STEPS, 1):
        if bit == 1:
            summary = summary + mark
        received = swapped(packed(summary, total, jnp.bfloat16), axis, mask)
        levels.append(received[:-8])
        their_state, their_decay = unpacked(received, heads)
        is_upper = here >> bit & 1 == 1
        upper.append(is_upper)
        lead.append(prefix)
        if bit == 1:
            summary = lax.dynamic_slice_in_dim(summary, odd * quarter, quarter)
            their_state = lax.dynamic_slice_in_dim(their_state, odd * quarter, quarter)
            start = start + odd * quarter
        if bit < len(STEPS):
            lower_state = jnp.where(is_upper, their_state, summary)
            upper_state = jnp.where(is_upper, summary, their_state)
            upper_decay = jnp.where(is_upper, total, their_decay)
            gain = lax.dynamic_slice_in_dim(jnp.exp(upper_decay), start, quarter)
            summary = gain[:, None, None] * lower_state + upper_state
            prefix = jnp.where(is_upper, prefix + their_decay, prefix)
            total = total + their_decay

    def joined(own, axis, place):
        theirs = swapped(own, axis, 1)
        pair = (jnp.where(place == 0, own, theirs), jnp.where(place == 0, theirs, own))
        return jnp.concatenate(pair, axis=1)

    def split(rows):
        return rows.reshape(1, -1, head_dim, rows.shape[1])

    near = joined(jnp.concatenate([split(levels[1]), split(levels[2])]), "z", odd)
    near = joined(jnp.concatenate([split(levels[0]), near]), "core", core)
    far = joined(jnp.concatenate([split(levels[3]), split(levels[4])]), "z", odd)
    far = joined(far, "core", core)
    all_levels = [first_level] + list(near) + list(far)
    mixed = local_mix(x_blk, b_blk, c_blk, running, mix[:inner] + levels[0][:1, :1] * 0)
    for rank, level in enumerate(all_levels):
        growth = jnp.where(upper[rank], jnp.exp(running + lead[rank][:, None]), 0.0)
        scale = (mix[inner + rank] * growth).T
        product = jnp.einsum("tn,hpn->thp", c_blk, level, preferred_element_type=jnp.float32)
        mixed = mixed + scale[:, :, None] * product
    mixed = mixed.reshape(tokens, width)
    gated = mixed * jax.nn.silu(gate_in[0].astype(jnp.float32))
    normed = (
        gated * lax.rsqrt(jnp.mean(gated * gated, axis=-1, keepdims=True) + EPS) * norm_gain
    ).astype(jnp.bfloat16)
    normed = lax.optimization_barrier(normed)
    dims = (((1,), (1,)), ((), ()))
    theirs = swapped(normed, "core", 1)
    rest_sent, rest_own = rest_product(theirs, normed, rest)
    rest_other = swapped(rest_sent, "core", 1)
    sent = lax.dot_general(theirs, main, dims, preferred_element_type=jnp.float32)
    other = swapped(sent, "core", 1)
    own = lax.dot_general(normed, main, dims, preferred_element_type=jnp.float32)
    order = column_order(lax.axis_index("dp"))
    return finished(core, own, other, rest_own, rest_other, order)[None]


def solution(mesh):
    whole = Mesh(mesh.devices.reshape(4, 8, 2, 4), ("x", "z", "core", "dp"))
    in_specs = (
        P("dp", SEQ, None),
        P("dp", SEQ, None),
        P("dp", SEQ, None),
        P("dp", SEQ, None),
        P("dp", None, SEQ),
        P("dp", None, None, SEQ),
        P(),
        P(None, SEQ + ("dp",)),
        P(None, SEQ + ("dp",)),
    )
    return jax.shard_map(
        per_device, mesh=whole, in_specs=in_specs, out_specs=P("dp", SEQ, None), check_vma=False
    )
```

```python
import jax
import jax.numpy as jnp
from jax import lax
from jax.experimental import pallas as pl
from jax.experimental.pallas import tpu as pltpu
from jax.sharding import Mesh
from jax.sharding import PartitionSpec as P

SPAN = 256
SPAN_BITS = 8
EPS = 1e-05
HIGH = lax.Precision.HIGHEST
SEQ = ("x", "z", "core")
STEPS = (("z", 1), ("z", 2), ("z", 4), ("x", 1), ("x", 2))
HEAD_DIM = 64
DIMS = (((1,), (1,)), ((), ()))


def swapped(value, axis, mask):
    return lax.ppermute(value, axis, [(i, i ^ mask) for i in range(lax.axis_size(axis))])


def shifted(value, axis, step):
    count = lax.axis_size(axis)
    return lax.ppermute(value, axis, [(i, (i + step) % count) for i in range(count)])


def top_bit(values):
    powers = jnp.arange(1, 31, dtype=jnp.int32)
    return jnp.sum(values[..., None] >> powers > 0, axis=-1)


def local_mix(x_blk, b_blk, c_blk, running, mix_low):
    length = running.shape[1]
    inner_count = mix_low.shape[0]
    position = jnp.arange(length, dtype=jnp.int32)
    differ = position[:, None] ^ position[None, :]
    level_table = jnp.where(differ > 0, top_bit(differ) + 1, 0)
    level_picks = (
        level_table[None] == jnp.arange(inner_count, dtype=jnp.int32)[:, None, None]
    ).astype(jnp.float32)
    chosen = jnp.einsum("lht,lts->hts", mix_low, level_picks, precision=HIGH)
    causal_mask = position[:, None] >= position[None, :]
    log_gap = jnp.where(causal_mask[None], running[:, :, None] - running[:, None, :], -jnp.inf)
    scores = jnp.dot(c_blk, b_blk.T, preferred_element_type=jnp.float32)
    weights = (chosen * jnp.exp(log_gap) * scores[None]).astype(jnp.bfloat16)
    return jnp.einsum("hts,shp->thp", weights, x_blk, preferred_element_type=jnp.float32)


def packed(state, decay, kind):
    heads, width, size = state.shape
    top = lax.reduce_precision(decay, 8, 7)
    middle = lax.reduce_precision(decay - top, 8, 7)
    low = lax.reduce_precision(decay - top - middle, 8, 7)
    tail = jnp.stack([top, middle, low] + [jnp.zeros_like(top)] * 5)
    tail = jnp.pad(tail, ((0, 0), (0, size - decay.shape[0])))
    rows = jnp.concatenate([state.reshape(heads * width, size), tail])
    return rows.astype(kind)


def unpacked(rows, heads):
    size = rows.shape[1]
    tail = rows[-8:, :heads].astype(jnp.float32)
    state = rows[:-8].reshape(-1, HEAD_DIM, size)
    return state.astype(jnp.float32), tail[0] + tail[1] + tail[2]


def gathered_weights(w_gate, w_up, core, row):
    gate, up = w_gate.T, w_up.T
    keep = jnp.where(core == 0, gate, up)
    other = swapped(jnp.where(core == 0, up, gate), "core", 1)
    pair = jnp.stack([jnp.where(core == 0, keep, other), jnp.where(core == 0, other, keep)])
    ring = [pair, shifted(pair, "dp", -1), shifted(pair, "dp", 2), shifted(pair, "dp", 1)]
    placed = []
    for index in range(4):
        turn = (index - row) % 4
        value = ring[0]
        for step in range(1, 4):
            value = jnp.where(turn == step, ring[step], value)
        placed.append(value)
    block = jnp.stack(placed, axis=1).reshape(-1, gate.shape[1])
    return lax.all_gather(block, ("x", "z"), axis=0, tiled=True)


def mix_kernel(local, first, near, far, c_blk, scales, gate_in, gain, out, gated, squares):
    step = pl.program_id(0)
    width = local.shape[1]
    heads = scales.shape[2]
    head = lax.broadcasted_iota(jnp.int32, (2 * heads, width), 0) & (heads - 1)
    lane = lax.broadcasted_iota(jnp.int32, (2 * heads, width), 1) + step * width
    spread = (head == lane >> 6).astype(jnp.float32).astype(jnp.bfloat16)
    levels = [first[...]] + [near[k] for k in range(3)] + [far[k] for k in range(2)]
    mixed = local[...]
    for rank, level in enumerate(levels):
        scale = scales[rank]
        top = scale.astype(jnp.bfloat16)
        low = (scale - top.astype(jnp.float32)).astype(jnp.bfloat16)
        both = jnp.concatenate([top, low], axis=1)
        wide = jnp.dot(both, spread, preferred_element_type=jnp.float32)
        product = lax.dot_general(c_blk[...], level, DIMS, preferred_element_type=jnp.float32)
        mixed = mixed + wide * product
    value = mixed * jax.nn.silu(gate_in[...].astype(jnp.float32))
    gated[:, pl.ds(pl.multiple_of(step * width, width), width)] = value
    part = jnp.sum(value * value, axis=1, keepdims=True)

    @pl.when(step == 0)
    def _():
        squares[...] = part

    @pl.when(step > 0)
    def _():
        squares[...] += part

    @pl.when(step == pl.num_programs(0) - 1)
    def _():
        rate = lax.rsqrt(squares[...] * (1.0 / out.shape[1]) + EPS)
        out[...] = (gated[...] * rate * gain[...]).astype(out.dtype)


def mixed_and_normed(local, first, near, far, c_blk, scales, gate_in, gain):
    tokens, width = local.shape
    size = c_blk.shape[1]
    cut = 256
    column = pl.BlockSpec((tokens, cut), lambda j: (0, j))
    return pl.pallas_call(
        mix_kernel,
        grid=(width // cut,),
        in_specs=[
            column,
            pl.BlockSpec((cut, size), lambda j: (j, 0)),
            pl.BlockSpec((3, cut, size), lambda j: (0, j, 0)),
            pl.BlockSpec((2, cut, size), lambda j: (0, j, 0)),
            pl.BlockSpec(c_blk.shape, lambda j: (0, 0)),
            pl.BlockSpec(scales.shape, lambda j: (0, 0, 0)),
            column,
            pl.BlockSpec((1, width), lambda j: (0, 0)),
        ],
        out_specs=pl.BlockSpec((tokens, width), lambda j: (0, 0)),
        out_shape=jax.ShapeDtypeStruct((tokens, width), jnp.bfloat16),
        scratch_shapes=[pltpu.VMEM((tokens, width), jnp.float32), pltpu.VMEM((tokens, 1), jnp.float32)],
        compiler_params=pltpu.CompilerParams(vmem_limit_bytes=32 * 2**20),
        cost_estimate=pl.CostEstimate(
            flops=14 * tokens * width * size, bytes_accessed=8 * 2**20, transcendentals=tokens * width
        ),
    )(local, first, near, far, c_blk, scales, gate_in, gain)


def per_device(x_in, gate_in, keys_b, queries_c, decay_log, level_mix, norm_gain, w_gate, w_up):
    tokens, width = x_in.shape[1:]
    heads = decay_log.shape[1]
    head_dim = HEAD_DIM
    inner = SPAN_BITS + 1
    core = lax.axis_index("core")
    here = (lax.axis_index("x") * lax.axis_size("z") + lax.axis_index("z")) * 2 + core
    mine = gathered_weights(w_gate, w_up, core, lax.axis_index("dp"))

    x_blk = x_in[0].reshape(tokens, heads, head_dim)
    b_blk, c_blk = keys_b[0], queries_c[0]
    mix = level_mix[0]
    running = jnp.cumsum(decay_log[0], axis=1)
    decay = running[:, -1]
    tail_decay = jnp.exp(running[:, -1:] - running)
    scaled_keys = (tail_decay.T[:, :, None] * b_blk[:, None, :]).astype(jnp.bfloat16)
    state = jnp.einsum("shn,shp->hpn", scaled_keys, x_blk, preferred_element_type=jnp.float32)

    half = heads // 2
    their_state, their_decay = unpacked(swapped(packed(state, decay, jnp.float32), "core", 1), heads)
    first_level = their_state.astype(jnp.bfloat16)
    lower_state = jnp.where(core == 0, state, their_state)
    upper_state = jnp.where(core == 0, their_state, state)
    upper_decay = jnp.where(core == 0, their_decay, decay)
    summary = jnp.exp(upper_decay)[:, None, None] * lower_state + upper_state
    summary = lax.dynamic_slice_in_dim(summary, core * half, half)
    total = decay + their_decay
    prefix = jnp.zeros_like(total)
    upper, lead = [core == 1], [prefix]
    prefix = jnp.where(core == 1, their_decay, 0.0)
    levels = []
    start = core * half
    quarter = half // 2
    odd = lax.axis_index("z") & 1
    for bit, (axis, mask) in enumerate(STEPS, 1):
        received = swapped(packed(summary, total, jnp.bfloat16), axis, mask)
        levels.append(received[:-8])
        their_state, their_decay = unpacked(received, heads)
        is_upper = here >> bit & 1 == 1
        upper.append(is_upper)
        lead.append(prefix)
        if bit == 1:
            summary = lax.dynamic_slice_in_dim(summary, odd * quarter, quarter)
            their_state = lax.dynamic_slice_in_dim(their_state, odd * quarter, quarter)
            start = start + odd * quarter
        if bit < len(STEPS):
            lower_state = jnp.where(is_upper, their_state, summary)
            upper_state = jnp.where(is_upper, summary, their_state)
            upper_decay = jnp.where(is_upper, total, their_decay)
            gain = lax.dynamic_slice_in_dim(jnp.exp(upper_decay), start, quarter)
            summary = gain[:, None, None] * lower_state + upper_state
            prefix = jnp.where(is_upper, prefix + their_decay, prefix)
            total = total + their_decay

    def joined(own, axis, place):
        theirs = swapped(own, axis, 1)
        pair = (jnp.where(place == 0, own, theirs), jnp.where(place == 0, theirs, own))
        return jnp.concatenate(pair, axis=1)

    def split(rows):
        return rows.reshape(1, -1, head_dim, rows.shape[1])

    near = joined(jnp.concatenate([split(levels[1]), split(levels[2])]), "z", odd)
    near = joined(jnp.concatenate([split(levels[0]), near]), "core", core)
    far = joined(jnp.concatenate([split(levels[3]), split(levels[4])]), "z", odd)
    far = joined(far, "core", core)
    local = local_mix(x_blk, b_blk, c_blk, running, mix[:inner] + levels[0][:1, :1] * 0)
    scales = []
    for rank in range(mix.shape[0] - inner):
        growth = jnp.where(upper[rank], jnp.exp(running + lead[rank][:, None]), 0.0)
        scales.append((mix[inner + rank] * growth).T)
    normed = mixed_and_normed(
        local.reshape(tokens, width),
        first_level.reshape(width, -1),
        near.reshape(3, width, -1),
        far.reshape(2, width, -1),
        c_blk,
        jnp.stack(scales),
        gate_in[0],
        norm_gain[None],
    )
    theirs = swapped(normed, "core", 1)
    sent = lax.dot_general(theirs, mine, DIMS, preferred_element_type=jnp.float32)
    other = swapped(sent, "core", 1)
    own = lax.dot_general(normed, mine, DIMS, preferred_element_type=jnp.float32)
    gate_pre = jnp.where(core == 0, own, other)
    up_pre = jnp.where(core == 0, other, own)
    return (jax.nn.silu(gate_pre) * up_pre).astype(jnp.bfloat16)[None]


def solution(mesh):
    whole = Mesh(mesh.devices.reshape(4, 8, 2, 4), ("x", "z", "core", "dp"))
    in_specs = (
        P("dp", SEQ, None),
        P("dp", SEQ, None),
        P("dp", SEQ, None),
        P("dp", SEQ, None),
        P("dp", None, SEQ),
        P("dp", None, None, SEQ),
        P(),
        P(None, SEQ + ("dp",)),
        P(None, SEQ + ("dp",)),
    )
    return jax.shard_map(
        per_device, mesh=whole, in_specs=in_specs, out_specs=P("dp", SEQ, None), check_vma=False
    )
```

```python
import jax
import jax.numpy as jnp
from jax import lax
from jax.experimental import pallas as pl
from jax.experimental.pallas import tpu as pltpu
from jax.sharding import Mesh
from jax.sharding import PartitionSpec as P

SPAN = 256
SPAN_BITS = 8
EPS = 1e-05
HIGH = lax.Precision.HIGHEST
SEQ = ("x", "z", "core")
STEPS = (("z", 1), ("z", 2), ("z", 4), ("x", 1), ("x", 2))
HEAD_DIM = 64
DIMS = (((1,), (1,)), ((), ()))


def swapped(value, axis, mask, senders=None):
    places = range(lax.axis_size(axis)) if senders is None else senders
    return lax.ppermute(value, axis, [(i, i ^ mask) for i in places])


def shifted(value, axis, step):
    count = lax.axis_size(axis)
    return lax.ppermute(value, axis, [(i, (i + step) % count) for i in range(count)])


def top_bit(values):
    powers = jnp.arange(1, 31, dtype=jnp.int32)
    return jnp.sum(values[..., None] >> powers > 0, axis=-1)


def local_mix(x_blk, b_blk, c_blk, running, mix_low):
    length = running.shape[1]
    inner_count = mix_low.shape[0]
    position = jnp.arange(length, dtype=jnp.int32)
    differ = position[:, None] ^ position[None, :]
    level_table = jnp.where(differ > 0, top_bit(differ) + 1, 0)
    level_picks = (
        level_table[None] == jnp.arange(inner_count, dtype=jnp.int32)[:, None, None]
    ).astype(jnp.float32)
    chosen = jnp.einsum("lht,lts->hts", mix_low, level_picks, precision=HIGH)
    causal_mask = position[:, None] >= position[None, :]
    log_gap = jnp.where(causal_mask[None], running[:, :, None] - running[:, None, :], -jnp.inf)
    scores = jnp.dot(c_blk, b_blk.T, preferred_element_type=jnp.float32)
    weights = (chosen * jnp.exp(log_gap) * scores[None]).astype(jnp.bfloat16)
    return jnp.einsum("hts,shp->thp", weights, x_blk, preferred_element_type=jnp.float32)


def packed(state, decay, kind):
    heads, width, size = state.shape
    top = lax.reduce_precision(decay, 8, 7)
    middle = lax.reduce_precision(decay - top, 8, 7)
    low = lax.reduce_precision(decay - top - middle, 8, 7)
    tail = jnp.stack([top, middle, low] + [jnp.zeros_like(top)] * 5)
    tail = jnp.pad(tail, ((0, 0), (0, size - decay.shape[0])))
    rows = jnp.concatenate([state.reshape(heads * width, size), tail])
    return rows.astype(kind)


def unpacked(rows, heads):
    size = rows.shape[1]
    tail = rows[-8:, :heads].astype(jnp.float32)
    state = rows[:-8].reshape(-1, HEAD_DIM, size)
    return state.astype(jnp.float32), tail[0] + tail[1] + tail[2]


def gathered_weights(w_gate, w_up, core, row):
    gate, up = w_gate.T, w_up.T
    keep = jnp.where(core == 0, gate, up)
    other = swapped(jnp.where(core == 0, up, gate), "core", 1)
    pair = jnp.stack([jnp.where(core == 0, keep, other), jnp.where(core == 0, other, keep)])
    ring = [pair, shifted(pair, "dp", -1), shifted(pair, "dp", 2), shifted(pair, "dp", 1)]
    placed = []
    for index in range(4):
        turn = (index - row) % 4
        value = ring[0]
        for step in range(1, 4):
            value = jnp.where(turn == step, ring[step], value)
        placed.append(value)
    block = jnp.stack(placed, axis=1).reshape(-1, gate.shape[1])
    return lax.all_gather(block, ("x", "z"), axis=0, tiled=True)


def mix_kernel(local, first, near, far, c_blk, scales, gate_in, gain, out, gated, squares):
    step = pl.program_id(0)
    width = local.shape[1]
    heads = scales.shape[2]
    head = lax.broadcasted_iota(jnp.int32, (2 * heads, width), 0) & (heads - 1)
    lane = lax.broadcasted_iota(jnp.int32, (2 * heads, width), 1) + step * width
    spread = (head == lane >> 6).astype(jnp.float32).astype(jnp.bfloat16)
    levels = [first[...]] + [near[k] for k in range(3)] + [far[k] for k in range(2)]
    mixed = local[...]
    for rank, level in enumerate(levels):
        scale = scales[rank]
        top = scale.astype(jnp.bfloat16)
        low = (scale - top.astype(jnp.float32)).astype(jnp.bfloat16)
        both = jnp.concatenate([top, low], axis=1)
        wide = jnp.dot(both, spread, preferred_element_type=jnp.float32)
        product = lax.dot_general(c_blk[...], level, DIMS, preferred_element_type=jnp.float32)
        mixed = mixed + wide * product
    value = mixed * jax.nn.silu(gate_in[...].astype(jnp.float32))
    gated[:, pl.ds(pl.multiple_of(step * width, width), width)] = value
    part = jnp.sum(value * value, axis=1, keepdims=True)

    @pl.when(step == 0)
    def _():
        squares[...] = part

    @pl.when(step > 0)
    def _():
        squares[...] += part

    @pl.when(step == pl.num_programs(0) - 1)
    def _():
        rate = lax.rsqrt(squares[...] * (1.0 / out.shape[1]) + EPS)
        out[...] = (gated[...] * rate * gain[...]).astype(out.dtype)


def mixed_and_normed(local, first, near, far, c_blk, scales, gate_in, gain):
    tokens, width = local.shape
    size = c_blk.shape[1]
    cut = 256
    column = pl.BlockSpec((tokens, cut), lambda j: (0, j))
    return pl.pallas_call(
        mix_kernel,
        grid=(width // cut,),
        in_specs=[
            column,
            pl.BlockSpec((cut, size), lambda j: (j, 0)),
            pl.BlockSpec((3, cut, size), lambda j: (0, j, 0)),
            pl.BlockSpec((2, cut, size), lambda j: (0, j, 0)),
            pl.BlockSpec(c_blk.shape, lambda j: (0, 0)),
            pl.BlockSpec(scales.shape, lambda j: (0, 0, 0)),
            column,
            pl.BlockSpec((1, width), lambda j: (0, 0)),
        ],
        out_specs=pl.BlockSpec((tokens, width), lambda j: (0, 0)),
        out_shape=jax.ShapeDtypeStruct((tokens, width), jnp.bfloat16),
        scratch_shapes=[pltpu.VMEM((tokens, width), jnp.float32), pltpu.VMEM((tokens, 1), jnp.float32)],
        compiler_params=pltpu.CompilerParams(vmem_limit_bytes=32 * 2**20),
        cost_estimate=pl.CostEstimate(
            flops=14 * tokens * width * size, bytes_accessed=8 * 2**20, transcendentals=tokens * width
        ),
    )(local, first, near, far, c_blk, scales, gate_in, gain)


def per_device(x_in, gate_in, keys_b, queries_c, decay_log, level_mix, norm_gain, w_gate, w_up):
    tokens, width = x_in.shape[1:]
    heads = decay_log.shape[1]
    head_dim = HEAD_DIM
    inner = SPAN_BITS + 1
    core = lax.axis_index("core")
    here = (lax.axis_index("x") * lax.axis_size("z") + lax.axis_index("z")) * 2 + core
    mine = gathered_weights(w_gate, w_up, core, lax.axis_index("dp"))

    x_blk = x_in[0].reshape(tokens, heads, head_dim)
    b_blk, c_blk = keys_b[0], queries_c[0]
    mix = level_mix[0]
    running = jnp.cumsum(decay_log[0], axis=1)
    decay = running[:, -1]
    tail_decay = jnp.exp(running[:, -1:] - running)
    scaled_keys = (tail_decay.T[:, :, None] * b_blk[:, None, :]).astype(jnp.bfloat16)
    state = jnp.einsum("shn,shp->hpn", scaled_keys, x_blk, preferred_element_type=jnp.float32)

    half = heads // 2
    their_state, their_decay = unpacked(swapped(packed(state, decay, jnp.float32), "core", 1), heads)
    first_level = their_state.astype(jnp.bfloat16)
    lower_state = jnp.where(core == 0, state, their_state)
    upper_state = jnp.where(core == 0, their_state, state)
    upper_decay = jnp.where(core == 0, their_decay, decay)
    summary = jnp.exp(upper_decay)[:, None, None] * lower_state + upper_state
    summary = lax.dynamic_slice_in_dim(summary, core * half, half)
    total = decay + their_decay
    prefix = jnp.zeros_like(total)
    upper, lead = [core == 1], [prefix]
    prefix = jnp.where(core == 1, their_decay, 0.0)
    levels = []
    start = core * half
    quarter = half // 2
    odd = lax.axis_index("z") & 1
    for bit, (axis, mask) in enumerate(STEPS, 1):
        senders = range(mask) if bit == len(STEPS) else None
        received = swapped(packed(summary, total, jnp.bfloat16), axis, mask, senders)
        levels.append(received[:-8])
        their_state, their_decay = unpacked(received, heads)
        is_upper = here >> bit & 1 == 1
        upper.append(is_upper)
        lead.append(prefix)
        if bit == 1:
            summary = lax.dynamic_slice_in_dim(summary, odd * quarter, quarter)
            their_state = lax.dynamic_slice_in_dim(their_state, odd * quarter, quarter)
            start = start + odd * quarter
        if bit < len(STEPS):
            lower_state = jnp.where(is_upper, their_state, summary)
            upper_state = jnp.where(is_upper, summary, their_state)
            upper_decay = jnp.where(is_upper, total, their_decay)
            gain = lax.dynamic_slice_in_dim(jnp.exp(upper_decay), start, quarter)
            summary = gain[:, None, None] * lower_state + upper_state
            prefix = jnp.where(is_upper, prefix + their_decay, prefix)
            total = total + their_decay

    def joined(own, axis, place, senders=None):
        theirs = swapped(own, axis, 1, senders)
        pair = (jnp.where(place == 0, own, theirs), jnp.where(place == 0, theirs, own))
        return jnp.concatenate(pair, axis=1)

    def split(rows):
        return rows.reshape(1, -1, head_dim, rows.shape[1])

    steps = range(2, lax.axis_size("z"))
    near = joined(jnp.concatenate([split(levels[1]), split(levels[2])]), "z", odd, steps)
    near = joined(jnp.concatenate([split(levels[0]), near]), "core", core)
    far = joined(jnp.concatenate([split(levels[3]), split(levels[4])]), "z", odd)
    far = joined(far, "core", core)
    local = local_mix(x_blk, b_blk, c_blk, running, mix[:inner] + levels[0][:1, :1] * 0)
    scales = []
    for rank in range(mix.shape[0] - inner):
        growth = jnp.where(upper[rank], jnp.exp(running + lead[rank][:, None]), 0.0)
        scales.append((mix[inner + rank] * growth).T)
    normed = mixed_and_normed(
        local.reshape(tokens, width),
        first_level.reshape(width, -1),
        near.reshape(3, width, -1),
        far.reshape(2, width, -1),
        c_blk,
        jnp.stack(scales),
        gate_in[0],
        norm_gain[None],
    )
    theirs = swapped(normed, "core", 1)
    sent = lax.dot_general(theirs, mine, DIMS, preferred_element_type=jnp.float32)
    other = swapped(sent, "core", 1)
    own = lax.dot_general(normed, mine, DIMS, preferred_element_type=jnp.float32)
    gate_pre = jnp.where(core == 0, own, other)
    up_pre = jnp.where(core == 0, other, own)
    return (jax.nn.silu(gate_pre) * up_pre).astype(jnp.bfloat16)[None]


def solution(mesh):
    whole = Mesh(mesh.devices.reshape(4, 8, 2, 4), ("x", "z", "core", "dp"))
    in_specs = (
        P("dp", SEQ, None),
        P("dp", SEQ, None),
        P("dp", SEQ, None),
        P("dp", SEQ, None),
        P("dp", None, SEQ),
        P("dp", None, None, SEQ),
        P(),
        P(None, SEQ + ("dp",)),
        P(None, SEQ + ("dp",)),
    )
    return jax.shard_map(
        per_device, mesh=whole, in_specs=in_specs, out_specs=P("dp", SEQ, None), check_vma=False
    )
```

```python
import jax
import jax.numpy as jnp
from jax import lax
from jax.experimental import pallas as pl
from jax.experimental.pallas import tpu as pltpu
from jax.sharding import Mesh
from jax.sharding import PartitionSpec as P

SPAN = 256
SPAN_BITS = 8
EPS = 1e-05
HIGH = lax.Precision.HIGHEST
SEQ = ("x", "z", "core")
STEPS = (("z", 1), ("z", 2), ("z", 4), ("x", 1), ("x", 2))
HEAD_DIM = 64
DIMS = (((1,), (1,)), ((), ()))


def swapped(value, axis, mask, senders=None):
    places = range(lax.axis_size(axis)) if senders is None else senders
    return lax.ppermute(value, axis, [(i, i ^ mask) for i in places])


def shifted(value, axis, step):
    count = lax.axis_size(axis)
    return lax.ppermute(value, axis, [(i, (i + step) % count) for i in range(count)])


def top_bit(values):
    powers = jnp.arange(1, 31, dtype=jnp.int32)
    return jnp.sum(values[..., None] >> powers > 0, axis=-1)


def local_mix(x_blk, b_blk, c_blk, running, mix_low):
    length = running.shape[1]
    inner_count = mix_low.shape[0]
    position = jnp.arange(length, dtype=jnp.int32)
    differ = position[:, None] ^ position[None, :]
    level_table = jnp.where(differ > 0, top_bit(differ) + 1, 0)
    level_picks = (
        level_table[None] == jnp.arange(inner_count, dtype=jnp.int32)[:, None, None]
    ).astype(jnp.float32)
    chosen = jnp.einsum("lht,lts->hts", mix_low, level_picks, precision=HIGH)
    causal_mask = position[:, None] >= position[None, :]
    log_gap = jnp.where(causal_mask[None], running[:, :, None] - running[:, None, :], -jnp.inf)
    scores = jnp.dot(c_blk, b_blk.T, preferred_element_type=jnp.float32)
    weights = (chosen * jnp.exp(log_gap) * scores[None]).astype(jnp.bfloat16)
    return jnp.einsum("hts,shp->thp", weights, x_blk, preferred_element_type=jnp.float32)


def packed(state, decay, kind):
    heads, width, size = state.shape
    top = lax.reduce_precision(decay, 8, 7)
    middle = lax.reduce_precision(decay - top, 8, 7)
    low = lax.reduce_precision(decay - top - middle, 8, 7)
    tail = jnp.stack([top, middle, low] + [jnp.zeros_like(top)] * 5)
    tail = jnp.pad(tail, ((0, 0), (0, size - decay.shape[0])))
    rows = jnp.concatenate([state.reshape(heads * width, size), tail])
    return rows.astype(kind)


def unpacked(rows, heads):
    size = rows.shape[1]
    tail = rows[-8:, :heads].astype(jnp.float32)
    state = rows[:-8].reshape(-1, HEAD_DIM, size)
    return state.astype(jnp.float32), tail[0] + tail[1] + tail[2]


def gathered_weights(w_gate, w_up, core, row):
    gate, up = w_gate.T, w_up.T
    keep = jnp.where(core == 0, gate, up)
    other = swapped(jnp.where(core == 0, up, gate), "core", 1)
    pair = jnp.stack([jnp.where(core == 0, keep, other), jnp.where(core == 0, other, keep)])
    ring = [pair, shifted(pair, "dp", -1), shifted(pair, "dp", 2), shifted(pair, "dp", 1)]
    placed = []
    for index in range(4):
        turn = (index - row) % 4
        value = ring[0]
        for step in range(1, 4):
            value = jnp.where(turn == step, ring[step], value)
        placed.append(value)
    block = jnp.stack(placed, axis=1).reshape(-1, gate.shape[1])
    return lax.all_gather(block, ("x", "z"), axis=0, tiled=True)


def mix_kernel(local, first, near, far, c_blk, scales, gate_in, gain, out, gated, squares):
    step = pl.program_id(0)
    width = local.shape[1]
    heads = scales.shape[2]
    head = lax.broadcasted_iota(jnp.int32, (2 * heads, width), 0) & (heads - 1)
    lane = lax.broadcasted_iota(jnp.int32, (2 * heads, width), 1) + step * width
    spread = (head == lane >> 6).astype(jnp.float32).astype(jnp.bfloat16)
    levels = [first[...]] + [near[k] for k in range(3)] + [far[k] for k in range(2)]
    mixed = local[...]
    for rank, level in enumerate(levels):
        scale = scales[rank]
        top = scale.astype(jnp.bfloat16)
        low = (scale - top.astype(jnp.float32)).astype(jnp.bfloat16)
        both = jnp.concatenate([top, low], axis=1)
        wide = jnp.dot(both, spread, preferred_element_type=jnp.float32)
        product = lax.dot_general(c_blk[...], level, DIMS, preferred_element_type=jnp.float32)
        mixed = mixed + wide * product
    value = mixed * jax.nn.silu(gate_in[...].astype(jnp.float32))
    gated[:, pl.ds(pl.multiple_of(step * width, width), width)] = value
    part = jnp.sum(value * value, axis=1, keepdims=True)

    @pl.when(step == 0)
    def _():
        squares[...] = part

    @pl.when(step > 0)
    def _():
        squares[...] += part

    @pl.when(step == pl.num_programs(0) - 1)
    def _():
        rate = lax.rsqrt(squares[...] * (1.0 / out.shape[1]) + EPS)
        out[...] = (gated[...] * rate * gain[...]).astype(out.dtype)


def mixed_and_normed(local, first, near, far, c_blk, scales, gate_in, gain):
    tokens, width = local.shape
    size = c_blk.shape[1]
    cut = 256
    column = pl.BlockSpec((tokens, cut), lambda j: (0, j))
    return pl.pallas_call(
        mix_kernel,
        grid=(width // cut,),
        in_specs=[
            column,
            pl.BlockSpec((cut, size), lambda j: (j, 0)),
            pl.BlockSpec((3, cut, size), lambda j: (0, j, 0)),
            pl.BlockSpec((2, cut, size), lambda j: (0, j, 0)),
            pl.BlockSpec(c_blk.shape, lambda j: (0, 0)),
            pl.BlockSpec(scales.shape, lambda j: (0, 0, 0)),
            column,
            pl.BlockSpec((1, width), lambda j: (0, 0)),
        ],
        out_specs=pl.BlockSpec((tokens, width), lambda j: (0, 0)),
        out_shape=jax.ShapeDtypeStruct((tokens, width), jnp.bfloat16),
        scratch_shapes=[pltpu.VMEM((tokens, width), jnp.float32), pltpu.VMEM((tokens, 1), jnp.float32)],
        compiler_params=pltpu.CompilerParams(vmem_limit_bytes=32 * 2**20),
        cost_estimate=pl.CostEstimate(
            flops=14 * tokens * width * size, bytes_accessed=8 * 2**20, transcendentals=tokens * width
        ),
    )(local, first, near, far, c_blk, scales, gate_in, gain)


def per_device(x_in, gate_in, keys_b, queries_c, decay_log, level_mix, norm_gain, w_gate, w_up):
    tokens, width = x_in.shape[1:]
    heads = decay_log.shape[1]
    head_dim = HEAD_DIM
    inner = SPAN_BITS + 1
    core = lax.axis_index("core")
    here = (lax.axis_index("x") * lax.axis_size("z") + lax.axis_index("z")) * 2 + core
    mine = gathered_weights(w_gate, w_up, core, lax.axis_index("dp"))

    x_blk = x_in[0].reshape(tokens, heads, head_dim)
    b_blk, c_blk = keys_b[0], queries_c[0]
    mix = level_mix[0]
    running = jnp.cumsum(decay_log[0], axis=1)
    decay = running[:, -1]
    tail_decay = jnp.exp(running[:, -1:] - running)
    scaled_keys = (tail_decay.T[:, :, None] * b_blk[:, None, :]).astype(jnp.bfloat16)
    state = jnp.einsum("shn,shp->hpn", scaled_keys, x_blk, preferred_element_type=jnp.float32)

    half = heads // 2
    their_state, their_decay = unpacked(swapped(packed(state, decay, jnp.float32), "core", 1), heads)
    first_level = their_state.astype(jnp.bfloat16)
    lower_state = jnp.where(core == 0, state, their_state)
    upper_state = jnp.where(core == 0, their_state, state)
    upper_decay = jnp.where(core == 0, their_decay, decay)
    summary = jnp.exp(upper_decay)[:, None, None] * lower_state + upper_state
    summary = lax.dynamic_slice_in_dim(summary, core * half, half)
    total = decay + their_decay
    prefix = jnp.zeros_like(total)
    upper, lead = [core == 1], [prefix]
    prefix = jnp.where(core == 1, their_decay, 0.0)
    levels = []
    start = core * half
    quarter = half // 2
    odd = lax.axis_index("z") & 1
    for bit, (axis, mask) in enumerate(STEPS, 1):
        senders = range(mask) if bit == len(STEPS) else range(3) if bit == len(STEPS) - 1 else None
        received = swapped(packed(summary, total, jnp.bfloat16), axis, mask, senders)
        levels.append(received[:-8])
        their_state, their_decay = unpacked(received, heads)
        is_upper = here >> bit & 1 == 1
        upper.append(is_upper)
        lead.append(prefix)
        if bit == 1:
            summary = lax.dynamic_slice_in_dim(summary, odd * quarter, quarter)
            their_state = lax.dynamic_slice_in_dim(their_state, odd * quarter, quarter)
            start = start + odd * quarter
        if bit < len(STEPS):
            lower_state = jnp.where(is_upper, their_state, summary)
            upper_state = jnp.where(is_upper, summary, their_state)
            upper_decay = jnp.where(is_upper, total, their_decay)
            gain = lax.dynamic_slice_in_dim(jnp.exp(upper_decay), start, quarter)
            summary = gain[:, None, None] * lower_state + upper_state
            prefix = jnp.where(is_upper, prefix + their_decay, prefix)
            total = total + their_decay

    def joined(own, axis, place, senders=None):
        theirs = swapped(own, axis, 1, senders)
        pair = (jnp.where(place == 0, own, theirs), jnp.where(place == 0, theirs, own))
        return jnp.concatenate(pair, axis=1)

    def split(rows):
        return rows.reshape(1, -1, head_dim, rows.shape[1])

    steps = range(2, lax.axis_size("z"))
    near = joined(jnp.concatenate([split(levels[1]), split(levels[2])]), "z", odd, steps)
    near = joined(jnp.concatenate([split(levels[0]), near]), "core", core)
    depth = lax.axis_size("z")
    steps = range(depth, lax.axis_size("x") * depth)
    far = joined(jnp.concatenate([split(levels[3]), split(levels[4])]), ("x", "z"), odd, steps)
    far = joined(far, "core", core)
    local = local_mix(x_blk, b_blk, c_blk, running, mix[:inner] + levels[0][:1, :1] * 0)
    scales = []
    for rank in range(mix.shape[0] - inner):
        growth = jnp.where(upper[rank], jnp.exp(running + lead[rank][:, None]), 0.0)
        scales.append((mix[inner + rank] * growth).T)
    normed = mixed_and_normed(
        local.reshape(tokens, width),
        first_level.reshape(width, -1),
        near.reshape(3, width, -1),
        far.reshape(2, width, -1),
        c_blk,
        jnp.stack(scales),
        gate_in[0],
        norm_gain[None],
    )
    theirs = swapped(normed, "core", 1)
    sent = lax.dot_general(theirs, mine, DIMS, preferred_element_type=jnp.float32)
    other = swapped(sent, "core", 1)
    own = lax.dot_general(normed, mine, DIMS, preferred_element_type=jnp.float32)
    gate_pre = jnp.where(core == 0, own, other)
    up_pre = jnp.where(core == 0, other, own)
    return (jax.nn.silu(gate_pre) * up_pre).astype(jnp.bfloat16)[None]


def solution(mesh):
    whole = Mesh(mesh.devices.reshape(4, 8, 2, 4), ("x", "z", "core", "dp"))
    in_specs = (
        P("dp", SEQ, None),
        P("dp", SEQ, None),
        P("dp", SEQ, None),
        P("dp", SEQ, None),
        P("dp", None, SEQ),
        P("dp", None, None, SEQ),
        P(),
        P(None, SEQ + ("dp",)),
        P(None, SEQ + ("dp",)),
    )
    return jax.shard_map(
        per_device, mesh=whole, in_specs=in_specs, out_specs=P("dp", SEQ, None), check_vma=False
    )
```
